256 devices in a mesh: grp: 4 (over y), row: 8 (over z), col: 8 (over x, core).
Axes of the slice: x: 4, y: 4, z: 8, core: 2. Of those that a mesh axis runs over, the one named last changes fastest.
Arguments:
- front: float32 [4, 8, 8, 8, 8, 128, 128], P('grp', 'row', None, 'col'), as said below
- child_update: float32 [4, 2, 8, 5, 8, 5, 128, 128], P('grp', None, 'row', None, 'col'), as said below
- child_tiles: int32 [4, 2, 40], replicated, may hold values from 0 to 63, as said below
Outputs:
- factored: float32 [4, 8, 8, 8, 8, 128, 128], P('grp', 'row', None, 'col')
The draws below stay inside these ranges and needn't reach their ends.
Inputs may be any that keep to these rules, and one draw needn't show every extreme that they name: `child_tiles`: each list holds 40 distinct front tiles in increasing order, exactly 5 of them of each residue modulo 8. `child_update`: each child update is a symmetric matrix over its listed tiles. Each front is symmetric, and with its children added the leading 5 * 128 square block is positive definite.
All inputs are finite; a program needn't handle non-finite values.
Results may differ from the reference program's by a relative error of at most 0.0001.
Values sent between devices are 32-bit elements; how exact they have to be, the bound alone decides.
No kernel may reach another device: no remote copies, remote signals or barrier semaphores. Data moves between devices by JAX's collectives and lax.ppermute only.
A program may use at most 128 MiB of HBM per device.

```python
import jax
import jax.numpy as jnp
from jax import lax

TILE_SIZE = 128
FRONT_TILES = 64
CHILD_TILES = 40
PANELS = 5
GROUPS = 4
ROW_TILES = 8
COL_TILES = 8
CHILD_ROWS = 5
CHILD_COLS = 5
RESIDUES = 8
PER_RESIDUE = 5
N_ROW = 8
N_COL = 8


def tile_sets(key):
    key = jax.random.fold_in(key, 11)
    slots = FRONT_TILES // RESIDUES
    scores = jax.random.randint(key, (GROUPS, 2, RESIDUES, slots), 0, 1 << 20)
    scores = scores * slots + jnp.arange(slots, dtype=jnp.int32)
    picked = jnp.argsort(scores, axis=-1)[..., :PER_RESIDUE].astype(jnp.int32)
    chosen = picked * RESIDUES + jnp.arange(RESIDUES, dtype=jnp.int32)[:, None]
    return jnp.sort(chosen.reshape(GROUPS, 2, CHILD_TILES), axis=-1).astype(jnp.int32)


def near_field(points, length_scale):
    count = points.shape[0]
    squared = jnp.zeros((count, count), jnp.float32)
    for axis_at in range(3):
        offset = points[:, axis_at][:, None] - points[:, axis_at][None, :]
        squared = squared + offset * offset
    return jnp.exp(-jnp.sqrt(squared) / length_scale)


def shaped_noise(key, size, exponent):
    raw = jax.random.uniform(key, (size, size), jnp.float32, -1.0, 1.0)
    raw = jnp.sign(raw) * jnp.abs(raw) ** exponent
    index = jnp.arange(size, dtype=jnp.int32)
    return jnp.where(index[:, None] < index[None, :], raw, raw.T)


def draw_child_tiles(key, part):
    return tile_sets(key)


def draw_child_update(key, part):
    listed = tile_sets(key)
    key = jax.random.fold_in(key, 5)
    spread = 1.0
    exponent = 1.0
    size = CHILD_TILES * TILE_SIZE
    index = jnp.arange(size, dtype=jnp.int32)

    def one_child(pair):
        sub, chosen = pair
        first, second = jax.random.split(sub)
        points = jax.random.uniform(first, (size, 3), jnp.float32) ** spread
        noise = shaped_noise(second, size, exponent) * 0.15
        tile_of = chosen[index // TILE_SIZE]
        leading = tile_of < PANELS
        inside = leading[:, None] & leading[None, :]
        matrix = 0.5 * near_field(points, 0.15) + jnp.where(inside, 0.0, noise)
        tiles = matrix.reshape(CHILD_TILES, TILE_SIZE, CHILD_TILES, TILE_SIZE).transpose(0, 2, 1, 3)
        row_order = jnp.argsort(chosen % N_ROW * FRONT_TILES + chosen).astype(jnp.int32)
        col_order = jnp.argsort(chosen % N_COL * FRONT_TILES + chosen).astype(jnp.int32)
        tiles = jnp.take(jnp.take(tiles, row_order, axis=0), col_order, axis=1)
        return tiles.reshape(N_ROW, CHILD_ROWS, N_COL, CHILD_COLS, TILE_SIZE, TILE_SIZE)
    subkeys = jax.random.split(key, GROUPS * 2)
    made = lax.map(one_child, (subkeys, listed.reshape(GROUPS * 2, CHILD_TILES)))
    return made.reshape(GROUPS, 2, N_ROW, CHILD_ROWS, N_COL, CHILD_COLS, TILE_SIZE, TILE_SIZE)


def draw_front(key, part):
    key = jax.random.fold_in(key, 7)
    spread = 1.0
    exponent = 1.0
    size = FRONT_TILES * TILE_SIZE
    lead = PANELS * TILE_SIZE
    index = jnp.arange(size, dtype=jnp.int32)
    outside = (index[:, None] >= lead) | (index[None, :] >= lead)
    diagonal = index[:, None] == index[None, :]

    def one_front(sub):
        first, second = jax.random.split(sub)
        points = jax.random.uniform(first, (size, 3), jnp.float32) ** spread
        noise = shaped_noise(second, size, exponent) * 0.15
        matrix = near_field(points, 0.15) + jnp.where(outside, noise, 0.0) + jnp.where(diagonal, 1.0, 0.0)
        tiles = matrix.reshape(FRONT_TILES, TILE_SIZE, FRONT_TILES, TILE_SIZE).transpose(0, 2, 1, 3)
        shaped = tiles.reshape(ROW_TILES, N_ROW, COL_TILES, N_COL, TILE_SIZE, TILE_SIZE)
        return shaped.transpose(1, 0, 3, 2, 4, 5)
    return lax.map(one_front, jax.random.split(key, GROUPS))


def setup_inputs(seed: int = 0) -> dict:
    streams_of = jax.random.split(jax.random.key(seed), 4)
    front = draw_front(jax.random.fold_in(streams_of[3], 71), 0)
    child_update = draw_child_update(jax.random.fold_in(streams_of[3], 71), 0)
    child_tiles = draw_child_tiles(jax.random.fold_in(streams_of[3], 71), 0)
    return dict(front=front, child_update=child_update, child_tiles=child_tiles)


def to_tiles(stored):
    return stored.transpose(1, 0, 3, 2, 4, 5).reshape(FRONT_TILES, FRONT_TILES, TILE_SIZE, TILE_SIZE)

def from_tiles(tiles):
    shaped = tiles.reshape(ROW_TILES, N_ROW, COL_TILES, N_COL, TILE_SIZE, TILE_SIZE)
    return shaped.transpose(1, 0, 3, 2, 4, 5)

def placed(listed, residues):
    keys = listed % residues * FRONT_TILES + listed
    return listed[jnp.argsort(keys)].astype(jnp.int32)

def factor(matrix):
    highest = lax.Precision.HIGHEST
    for step in range(PANELS):
        lo = step * TILE_SIZE
        hi = lo + TILE_SIZE
        lower = jnp.linalg.cholesky(matrix[lo:hi, lo:hi])
        inverse = jax.scipy.linalg.solve_triangular(lower, jnp.eye(TILE_SIZE, dtype=matrix.dtype), lower=True)
        column = jnp.dot(matrix[hi:, lo:hi], inverse.T, precision=highest)
        rowpart = jnp.dot(inverse, matrix[lo:hi, hi:], precision=highest)
        trailing = matrix[hi:, hi:] - jnp.dot(column, rowpart, precision=highest)
        matrix = matrix.at[hi:, hi:].set(trailing)
        matrix = matrix.at[hi:, lo:hi].set(column).at[lo:hi, hi:].set(rowpart)
        matrix = matrix.at[lo:hi, lo:hi].set(lower)
    return matrix

def reference(front, child_update, child_tiles):
    size = FRONT_TILES * TILE_SIZE
    results = []
    for group in range(GROUPS):
        tiles = to_tiles(front[group])
        for slot, source in ((0, group), (1, group ^ 1)):
            listed = child_tiles[source, slot]
            rows_at = placed(listed, N_ROW)
            cols_at = placed(listed, N_COL)
            block = child_update[source, slot].reshape(CHILD_TILES, CHILD_TILES, TILE_SIZE, TILE_SIZE)
            tiles = tiles.at[rows_at[:, None], cols_at[None, :]].add(block)
        matrix = tiles.transpose(0, 2, 1, 3).reshape(size, size)
        matrix = factor(matrix)
        tiles = matrix.reshape(FRONT_TILES, TILE_SIZE, FRONT_TILES, TILE_SIZE).transpose(0, 2, 1, 3)
        results.append(from_tiles(tiles))
    return jnp.stack(results)
```

```python
import functools

import jax
import jax.numpy as jnp
from jax import lax
from jax.experimental import pallas as pl
from jax.experimental.pallas import tpu as pltpu
from jax.sharding import PartitionSpec as P

PANELS = 5
TILE = 128
LEAD = PANELS * TILE
BLOCK = 32
SLOTS = 3
HIGHEST = lax.Precision.HIGHEST
VMEM = pltpu.VMEM
SMEM = pltpu.SMEM


def mul_nn(a, b, precision=HIGHEST):
    return lax.dot_general(
        a, b, (((1,), (0,)), ((), ())), precision=precision, preferred_element_type=jnp.float32
    )


def mul_tn(a, b, precision=HIGHEST):
    return lax.dot_general(
        a, b, (((0,), (0,)), ((), ())), precision=precision, preferred_element_type=jnp.float32
    )


def mul_nt(a, b, precision=HIGHEST):
    return lax.dot_general(
        a, b, (((1,), (1,)), ((), ())), precision=precision, preferred_element_type=jnp.float32
    )


def over_rows(x, at):
    return jnp.broadcast_to(x[at : at + 1, :], (8, TILE))


def eliminate(v, w, base):
    parts = BLOCK // 8
    sub = lax.broadcasted_iota(jnp.int32, (8, TILE), 0)
    cols = [
        [jnp.broadcast_to(v[h][:, base + j : base + j + 1], (8, TILE)) for h in range(parts)]
        for j in range(BLOCK)
    ]
    scale = [jnp.zeros((8, TILE), jnp.float32) for _ in range(parts)]
    for j in range(BLOCK):
        top, at = divmod(j, 8)
        root = lax.rsqrt(over_rows(cols[j][top], at))
        inverse = root * root
        scale[top] = jnp.where(sub == at, root, scale[top])
        v_row = over_rows(v[top], at)
        w_row = over_rows(w[top], at)
        c_row = {k: over_rows(cols[k][top], at) for k in range(j + 1, BLOCK)}
        for h in range(top, parts):
            if h == top and at == 7:
                continue
            factor = cols[j][h] * inverse
            if h == top:
                factor = jnp.where(sub > at, factor, 0.0)
            v[h] = v[h] - factor * v_row
            w[h] = w[h] - factor * w_row
            for k in range(j + 1, BLOCK):
                cols[k][h] = cols[k][h] - factor * c_row[k]
    upper = jnp.concatenate([x * s for x, s in zip(v, scale)], axis=0)
    lower_inverse = jnp.concatenate([x * s for x, s in zip(w, scale)], axis=0)
    return upper, lower_inverse


def factor_tile(pivot):
    row = lax.broadcasted_iota(jnp.int32, (TILE, TILE), 0)
    col = lax.broadcasted_iota(jnp.int32, (TILE, TILE), 1)
    rest = jnp.concatenate([pivot, (row == col).astype(jnp.float32)], axis=1)
    uppers, inverses = [], []
    for base in range(0, TILE, BLOCK):
        v = [rest[at : at + 8, :TILE] for at in range(0, BLOCK, 8)]
        w = [rest[at : at + 8, TILE:] for at in range(0, BLOCK, 8)]
        upper, inverse = eliminate(v, w, base)
        uppers.append(upper)
        inverses.append(inverse)
        if base + BLOCK < TILE:
            update = mul_tn(upper, jnp.concatenate([upper, inverse], axis=1))
            rest = rest[BLOCK:] - update[base + BLOCK :]
    upper = jnp.where(row <= col, jnp.concatenate(uppers, axis=0), 0.0)
    inverse = jnp.where(row >= col, jnp.concatenate(inverses, axis=0), 0.0)
    return upper, inverse


def factor_kernel(place, mine, other, inverse_ref, diagonal_ref, work):
    half = place[1] % 2
    chip = place[1] // 2

    def stored(column, slot):
        away = lax.rem(chip + 4 - column // 2, 4)
        here = mine[away, slot]
        there = other[away, slot]
        return jnp.where(half == column % 2, here, there)

    def span(at):
        return slice(at * TILE, (at + 1) * TILE)

    for k in range(PANELS):
        for i in range(k, PANELS):
            apart = i - k
            if apart < SLOTS:
                tile = stored(i, apart)
            else:
                tile = stored(k, PANELS - apart).T
            work[span(k), span(i)] = tile
    for k in range(PANELS):
        upper, inverse = factor_tile(work[span(k), span(k)])
        diagonal_ref[k] = upper.T
        work[span(k), span(PANELS + k)] = inverse
        if k + 1 < PANELS:
            wide = slice((k + 1) * TILE, (k + 1) * TILE + 4 * TILE)
            work[span(k), wide] = mul_nn(inverse, work[span(k), wide])
        else:
            wide = slice(LEAD, LEAD + 4 * TILE)
            work[span(k), wide] = mul_nn(inverse, work[span(k), wide])
        for i in range(k + 1, PANELS):
            old = slice(i * TILE, LEAD + k * TILE)
            new = span(PANELS + k)
            left = work[span(k), span(i)]
            both = mul_tn(left, work[span(k), i * TILE : LEAD + (k + 1) * TILE])
            width = LEAD + k * TILE - i * TILE
            work[span(i), old] = work[span(i), old] - both[:, :width]
            work[span(i), new] = -both[:, width:]
    for k in range(PANELS):
        done = (k + 1) * TILE
        inverse_ref[span(k), :done] = work[span(k), LEAD : LEAD + done]
        if done < LEAD:
            inverse_ref[span(k), done:] = jnp.zeros((TILE, LEAD - done), jnp.float32)


def pick_kernel(place, own, first, second, fourth, sixth, out):
    row = place[0]
    column = place[1]
    for slot in range(SLOTS):
        wanted = lax.rem(column + 2 * PANELS - slot, PANELS)
        away = lax.rem(row + 8 - wanted, 8)
        sources = [own, first]
        sources += [ref.at[part] for ref in (second, fourth, sixth) for part in range(2)]
        for at, ref in enumerate(sources):

            @pl.when(away == at)
            def _():
                out[slot] = ref[...]


def panel_kernel(pos, front_row, front_col, own_row, own_col, corner, sides, row_out, col_out):
    row_out[...] = front_row[0]
    col_out[...] = front_col[:, 0]
    for m in range(8):
        u = pos[0, 1, m]

        @pl.when((pos[0, 0, 0] == 0) & (u >= 0))
        def _():
            row_out[m] += own_row[0, u]

        t = pos[0, 0, m]

        @pl.when((pos[0, 1, 0] == 0) & (t >= 0))
        def _():
            col_out[m] += own_col[t, 0]

        u2 = pos[1, 1, m]
        t2 = pos[1, 0, m]

        @pl.when((pos[1, 0, 0] == 0) & (u2 == 0))
        def _():
            row_out[m] += corner[...]

        @pl.when((pos[1, 0, 0] == 0) & (u2 > 0))
        def _():
            row_out[m] += sides[u2 - 1]

        @pl.when((pos[1, 1, 0] == 0) & (t2 == 0))
        def _():
            col_out[m] += corner[...]

        @pl.when((pos[1, 1, 0] == 0) & (t2 > 0))
        def _():
            col_out[m] += sides[4 + t2 - 1]


def split(x):
    high = x.astype(jnp.bfloat16)
    low = (x - high.astype(jnp.float32)).astype(jnp.bfloat16)
    return high, low


def schur_kernel(
    pos, place, front, own, corner, sides, inner, row_tiles, mine, other, inverse, diagonal, out,
    panel, c_full, c_high, c_low, r_full, r_high, r_low,
):
    line = pl.program_id(0)
    row = place[0]
    column = place[1]

    @pl.when(line == 0)
    def _():
        half = column % 2
        chip = column // 2
        for k in range(PANELS):
            away = lax.rem(chip + 4 - k // 2, 4)

            @pl.when(half == k % 2)
            def _():
                panel[:, k * TILE : (k + 1) * TILE] = mine[away].reshape(8 * TILE, TILE)

            @pl.when(half != k % 2)
            def _():
                panel[:, k * TILE : (k + 1) * TILE] = other[away].reshape(8 * TILE, TILE)

        for k in range(PANELS):
            done = (k + 1) * TILE
            here = slice(k * TILE, done)
            part = mul_nt(panel[:, :done], inverse[here, :done])
            high, low = split(part)
            c_high[:, here] = high
            c_low[:, here] = low
            c_full[k] = part.reshape(8, TILE, TILE)
            for m in range(8):
                rows = row_tiles[: k + 1, m].reshape(done, TILE)
                part = mul_nn(inverse[here, :done], rows)
                high, low = split(part)
                there = slice(m * TILE, (m + 1) * TILE)
                r_high[here, there] = high
                r_low[here, there] = low
                r_full[k, m] = part

    at = pl.ds(pl.multiple_of(line * TILE, TILE), TILE)
    left_high = c_high[at, :]
    left_low = c_low[at, :]
    right_high = r_high[...]
    update = mul_nn(left_high, right_high, None)
    update += mul_nn(left_high, r_low[...], None)
    update += mul_nn(left_low, right_high, None)
    t = pos[0, 0, line]
    t2 = pos[1, 0, line]
    for m in range(8):
        out[0, m] = front[0, m] - update[:, m * TILE : (m + 1) * TILE]
        u = pos[0, 1, m]
        u2 = pos[1, 1, m]

        @pl.when((t >= 0) & (u >= 0))
        def _():
            out[0, m] += own[t, u]

        @pl.when((t2 == 0) & (u2 == 0))
        def _():
            out[0, m] += corner[...]

        @pl.when((t2 == 0) & (u2 > 0))
        def _():
            out[0, m] += sides[u2 - 1]

        @pl.when((t2 > 0) & (u2 == 0))
        def _():
            out[0, m] += sides[4 + t2 - 1]

        @pl.when((t2 > 0) & (u2 > 0))
        def _():
            out[0, m] += inner[t2 - 1, u2 - 1]

    in_row = (line == 0) & (row < PANELS)

    @pl.when((column < PANELS) & jnp.logical_not(in_row & (row <= column)))
    def _():
        out[0, 0] = c_full[jnp.minimum(column, PANELS - 1), line]

    @pl.when(in_row)
    def _():
        pivot = jnp.minimum(row, PANELS - 1)
        for m in range(1, 8):
            out[0, m] = r_full[pivot, m]

        @pl.when(row < column)
        def _():
            out[0, 0] = r_full[pivot, 0]

        @pl.when(row == column)
        def _():
            out[0, 0] = diagonal[pivot]


def whole(*shape):
    return pl.BlockSpec(shape, lambda *_: (0,) * len(shape))


def f32(*shape):
    return jax.ShapeDtypeStruct(shape, jnp.float32)


def places(lists, position, count):
    value = jnp.arange(count, dtype=jnp.int32) * 8 + position
    there = jnp.any(lists[:, None, :] == value[None, :, None], axis=2)
    same = (lists % 8 == position)[:, None, :]
    before = jnp.sum((lists[:, None, :] < value[None, :, None]) & same, axis=2, dtype=jnp.int32)
    return jnp.where(there, before, -1)


def sources(column):
    return [(column - slot) % PANELS for slot in range(SLOTS)]


def per_device(front, child_update, child_tiles):
    row_at = lax.axis_index("row")
    col_at = lax.axis_index("col")
    group_at = lax.axis_index("grp")
    local = front[0, 0, :, 0]
    own = child_update[0, 0, 0, :, 0]
    given = child_update[0, 1, 0, :, 0]
    both = ("row", "col")
    limit = pltpu.CompilerParams(vmem_limit_bytes=56 * 1024 * 1024)

    siblings = [(g, g ^ 1) for g in range(4)]
    corner = lax.ppermute(given[0, 0], "grp", siblings)
    sides = lax.ppermute(jnp.concatenate([given[0, 1:], given[1:, 0]], axis=0), "grp", siblings)
    inner = lax.ppermute(given[1:, 1:], "grp", siblings)

    lists = jnp.stack([child_tiles[group_at, 0], child_tiles[jnp.bitwise_xor(group_at, 1), 1]])
    pos = jnp.stack([places(lists, row_at, 8), places(lists, col_at, 8)], axis=1)
    place = jnp.stack([row_at, col_at]).astype(jnp.int32)

    first = (pos[:, 0, 0] == 0) & (pos[:, 1, 0] == 0)
    tile = local[0, 0] + jnp.where(first[0], own[0, 0], 0.0) + jnp.where(first[1], corner, 0.0)

    step = [
        (z * 8 + c, (z + 1) % 8 * 8 + c) for c in range(PANELS) for z in sources(c)
    ]
    up = lax.ppermute(tile, both, step)
    pair = jnp.stack([tile, up])
    spread = []
    for away in (2, 4, 6):
        holders = {(z + d) % 8 for d in range(2) for z in range(PANELS)}
        step = [
            (z * 8 + c, (z + away) % 8 * 8 + c)
            for c in range(PANELS)
            for z in sorted({(s + d) % 8 for s in sources(c) for d in range(2)})
        ]
        spread.append(lax.ppermute(pair, both, step))
    picked = pl.pallas_call(
        pick_kernel,
        out_shape=f32(SLOTS, TILE, TILE),
        in_specs=[pl.BlockSpec(memory_space=SMEM)] + [pl.BlockSpec(memory_space=VMEM)] * 5,
        out_specs=pl.BlockSpec(memory_space=VMEM),
        name="pick",
    )(place, tile, up, *spread)
    mine = [picked]
    for away in (2, 4, 6):
        mine.append(
            lax.ppermute(picked, "col", [(c, (c + away) % 8) for c in range(PANELS)])
        )
    mine = jnp.stack(mine)
    across = [(c, c ^ 1) for c in range(8)]
    other = lax.ppermute(mine, "col", across)
    inverse, diagonal = pl.pallas_call(
        factor_kernel,
        out_shape=[f32(LEAD, LEAD), f32(PANELS, TILE, TILE)],
        in_specs=[pl.BlockSpec(memory_space=SMEM)] + [pl.BlockSpec(memory_space=VMEM)] * 2,
        out_specs=[pl.BlockSpec(memory_space=VMEM)] * 2,
        scratch_shapes=[pltpu.VMEM((LEAD, 2 * LEAD), jnp.float32)],
        compiler_params=limit,
        cost_estimate=pl.CostEstimate(
            flops=40_000_000_000, bytes_accessed=6_000_000, transcendentals=0
        ),
        name="factor",
    )(place, mine, other)

    row_panel, col_panel = pl.pallas_call(
        panel_kernel,
        grid=(1,),
        out_shape=[f32(8, TILE, TILE)] * 2,
        in_specs=[
            pl.BlockSpec(memory_space=SMEM),
            whole(1, 8, TILE, TILE),
            whole(8, 1, TILE, TILE),
            whole(1, 5, TILE, TILE),
            whole(5, 1, TILE, TILE),
            whole(TILE, TILE),
            whole(8, TILE, TILE),
        ],
        out_specs=[whole(8, TILE, TILE)] * 2,
        name="panels",
    )(pos, local, local, own, own, corner, sides)

    row_tiles = lax.all_gather(row_panel, "row")
    col_mine = [col_panel]
    for away in (2, 4, 6):
        col_mine.append(
            lax.ppermute(col_panel, "col", [(c, (c + away) % 8) for c in range(PANELS)])
        )
    col_mine = jnp.stack(col_mine)
    col_other = lax.ppermute(col_mine, "col", across)

    result = pl.pallas_call(
        schur_kernel,
        grid=(8,),
        out_shape=f32(8, 8, TILE, TILE),
        in_specs=[
            pl.BlockSpec(memory_space=SMEM),
            pl.BlockSpec(memory_space=SMEM),
            pl.BlockSpec((1, 8, TILE, TILE), lambda i: (i, 0, 0, 0)),
            whole(5, 5, TILE, TILE),
            whole(TILE, TILE),
            whole(8, TILE, TILE),
            whole(4, 4, TILE, TILE),
            whole(PANELS, 8, TILE, TILE),
            whole(4, 8, TILE, TILE),
            whole(4, 8, TILE, TILE),
            whole(LEAD, LEAD),
            whole(PANELS, TILE, TILE),
        ],
        out_specs=pl.BlockSpec((1, 8, TILE, TILE), lambda i: (i, 0, 0, 0)),
        scratch_shapes=[
            pltpu.VMEM((8 * TILE, LEAD), jnp.float32),
            pltpu.VMEM((PANELS, 8, TILE, TILE), jnp.float32),
            pltpu.VMEM((8 * TILE, LEAD), jnp.bfloat16),
            pltpu.VMEM((8 * TILE, LEAD), jnp.bfloat16),
            pltpu.VMEM((PANELS, 8, TILE, TILE), jnp.float32),
            pltpu.VMEM((LEAD, 8 * TILE), jnp.bfloat16),
            pltpu.VMEM((LEAD, 8 * TILE), jnp.bfloat16),
        ],
        compiler_params=limit,
        name="schur",
    )(
        pos, place, local, own, corner, sides, inner, row_tiles, col_mine, col_other,
        inverse, diagonal,
    )
    return result[None, None, :, None]


def solution(mesh):
    in_specs = (
        P("grp", "row", None, "col", None, None, None),
        P("grp", None, "row", None, "col", None, None, None),
        P(),
    )
    out_specs = P("grp", "row", None, "col", None, None, None)
    return jax.shard_map(
        per_device, mesh=mesh, in_specs=in_specs, out_specs=out_specs, check_vma=False
    )
```

```python
import functools

import jax
import jax.numpy as jnp
from jax import lax
from jax.experimental import pallas as pl
from jax.experimental.pallas import tpu as pltpu
from jax.sharding import PartitionSpec as P

PANELS = 5
TILE = 128
LEAD = PANELS * TILE
BLOCK = 32
SUB = 16
SLOTS = 3
HEAD = 3
WIDTH = 2
CUTS = ((0, 256), (256, 512), (512, 640))
HIGHEST = lax.Precision.HIGHEST
VMEM = pltpu.VMEM
SMEM = pltpu.SMEM


def mul_nn(a, b, precision=HIGHEST):
    return lax.dot_general(
        a, b, (((1,), (0,)), ((), ())), precision=precision, preferred_element_type=jnp.float32
    )


def mul_tn(a, b, precision=HIGHEST):
    return lax.dot_general(
        a, b, (((0,), (0,)), ((), ())), precision=precision, preferred_element_type=jnp.float32
    )


def mul_nt(a, b, precision=HIGHEST):
    return lax.dot_general(
        a, b, (((1,), (1,)), ((), ())), precision=precision, preferred_element_type=jnp.float32
    )


def over_rows(x, at):
    return jnp.broadcast_to(x[at : at + 1, :], (8, TILE))


def eliminate(v, w, base):
    parts = BLOCK // 8
    sub = lax.broadcasted_iota(jnp.int32, (8, TILE), 0)
    scale = [jnp.zeros((8, TILE), jnp.float32) for _ in range(parts)]
    cols = {}
    for j in range(BLOCK):
        top, at = divmod(j, 8)
        group = range(j + 1, (j // SUB + 1) * SUB)
        if j % SUB == 0:
            cols = {
                k: [
                    jnp.broadcast_to(v[h][:, base + k : base + k + 1], (8, TILE))
                    if h >= top
                    else None
                    for h in range(parts)
                ]
                for k in range(j, j + SUB)
            }
        root = lax.rsqrt(over_rows(cols[j][top], at))
        inverse = root * root
        scale[top] = jnp.where(sub == at, root, scale[top])
        v_row = over_rows(v[top], at)
        w_row = over_rows(w[top], at)
        c_row = {k: over_rows(cols[k][top], at) for k in group}
        for h in range(top, parts):
            if h == top and at == 7:
                continue
            factor = cols[j][h] * inverse
            if h == top:
                factor = jnp.where(sub > at, factor, 0.0)
            for k in group:
                cols[k][h] = cols[k][h] - factor * c_row[k]
            v[h] = v[h] - factor * v_row
            w[h] = w[h] - factor * w_row
    upper = jnp.concatenate([x * s for x, s in zip(v, scale)], axis=0)
    lower_inverse = jnp.concatenate([x * s for x, s in zip(w, scale)], axis=0)
    return upper, lower_inverse


def factor_tile(pivot, beside=()):
    beside = list(beside)
    row = lax.broadcasted_iota(jnp.int32, (TILE, TILE), 0)
    col = lax.broadcasted_iota(jnp.int32, (TILE, TILE), 1)
    rest = jnp.concatenate([pivot, (row == col).astype(jnp.float32)], axis=1)
    uppers, inverses = [], []
    blocks = TILE // BLOCK
    share = -(-len(beside) // blocks)
    for base in range(0, TILE, BLOCK):
        for _ in range(min(share, len(beside))):
            beside.pop(0)()
        v = [rest[at : at + 8, :TILE] for at in range(0, BLOCK, 8)]
        w = [rest[at : at + 8, TILE:] for at in range(0, BLOCK, 8)]
        upper, inverse = eliminate(v, w, base)
        uppers.append(upper)
        inverses.append(inverse)
        if base + BLOCK < TILE:
            update = mul_tn(upper, jnp.concatenate([upper, inverse], axis=1))
            rest = rest[BLOCK:] - update[base + BLOCK :]
    upper = jnp.where(row <= col, jnp.concatenate(uppers, axis=0), 0.0)
    inverse = jnp.where(row >= col, jnp.concatenate(inverses, axis=0), 0.0)
    return upper, inverse


def span(at):
    return slice(at * TILE, (at + 1) * TILE)


def advance(work, diagonal, k, beside=()):
    upper, inverse = factor_tile(work[span(k), span(k)], beside)
    diagonal[k] = upper.T
    work[span(k), span(PANELS + k)] = inverse
    at = min(k + 1, PANELS) * TILE
    wide = slice(at, at + (PANELS - 1) * TILE)
    work[span(k), wide] = mul_nn(inverse, work[span(k), wide])
    for i in range(k + 1, PANELS):
        old = slice(i * TILE, LEAD + k * TILE)
        both = mul_tn(work[span(k), span(i)], work[span(k), i * TILE : LEAD + (k + 1) * TILE])
        width = LEAD + k * TILE - i * TILE
        work[span(i), old] = work[span(i), old] - both[:, :width]
        work[span(i), span(PANELS + k)] = -both[:, width:]


def keep_inverse(work, inverse_ref, k):
    done = (k + 1) * TILE
    inverse_ref[span(k), :done] = work[span(k), LEAD : LEAD + done]
    if done < LEAD:
        inverse_ref[span(k), done:] = jnp.zeros((TILE, LEAD - done), jnp.float32)


def head_kernel(place, mine, other, inverse_ref, diagonal_ref, rest_ref, work):
    half = place[1] % 2
    chip = place[1] // 2

    def stored(column, slot):
        away = lax.rem(chip + 4 - column // 2, 4)
        here = mine[away, slot]
        there = other[away, slot]
        return jnp.where(half == column % 2, here, there)

    for k in range(PANELS):
        for i in range(k, PANELS):
            apart = i - k
            if apart < SLOTS:
                tile = stored(i, apart)
            else:
                tile = stored(k, PANELS - apart).T
            work[span(k), span(i)] = tile
    for k in range(HEAD):
        advance(work, diagonal_ref, k)
        keep_inverse(work, inverse_ref, k)
    rest_ref[...] = work[HEAD * TILE :, HEAD * TILE : LEAD + HEAD * TILE]


def tail_kernel(
    place, rest, head_inverse, head_diagonal, m0, m1, m2, m3, o0, o1, o2, o3,
    inverse_ref, diagonal_ref, high, low, own_column, work, panel, full,
):
    column = place[1]
    half = column % 2
    chip = column // 2
    for k in range(PANELS):
        away = lax.rem(chip + 4 - k // 2, 4)
        for at, (mine, other) in enumerate(((m0, o0), (m1, o1), (m2, o2), (m3, o3))):

            @pl.when((away == at) & (half == k % 2))
            def _():
                panel[:, k * TILE : (k + 1) * TILE] = mine[...].reshape(8 * TILE, TILE)

            @pl.when((away == at) & (half != k % 2))
            def _():
                panel[:, k * TILE : (k + 1) * TILE] = other[...].reshape(8 * TILE, TILE)

    work[HEAD * TILE :, HEAD * TILE : LEAD + HEAD * TILE] = rest[...]
    inverse_ref[: HEAD * TILE] = head_inverse[...]
    diagonal_ref[:HEAD] = head_diagonal[...]

    def product(rows, at, end):
        part = mul_nt(panel[rows, :end], inverse_ref[at:end, :end])
        high[rows, at:end], low[rows, at:end] = split(part)
        full[rows, at:end] = part

    quarters = [slice(at, at + 2 * TILE) for at in range(0, 8 * TILE, 2 * TILE)]
    for k in range(HEAD, PANELS):
        start, stop = CUTS[k - HEAD]
        beside = [functools.partial(product, rows, start, stop) for rows in quarters]
        advance(work, diagonal_ref, k, beside)
        keep_inverse(work, inverse_ref, k)
    product(slice(0, 8 * TILE), *CUTS[-1])
    wanted = jnp.minimum(column, PANELS - 1)
    for k in range(PANELS):

        @pl.when(wanted == k)
        def _():
            own_column[...] = full[:, k * TILE : (k + 1) * TILE].reshape(8, TILE, TILE)


def pick_kernel(place, *refs):
    *found, out = refs
    for slot in range(SLOTS):
        wanted = lax.rem(place[1] + 2 * PANELS - slot, PANELS)
        away = lax.rem(place[0] + 8 - wanted, 8)
        for at, ref in enumerate(found):

            @pl.when(away == at)
            def _():
                out[slot] = ref[...]


def tile_kernel(pos, front, own, given, out):
    out[...] = front[0, 0]
    for s, child in ((0, own), (1, given)):

        @pl.when((pos[s, 0, 0] == 0) & (pos[s, 1, 0] == 0))
        def _():
            out[...] += child[0, 0]


def row_kernel(pos, front, own, given, out):
    out[...] = front[0]
    for s, child in ((0, own), (1, given)):
        for m in range(8):
            u = pos[s, 1, m]

            @pl.when((pos[s, 0, 0] == 0) & (u >= 0))
            def _():
                out[m] += child[0, u]


def col_kernel(pos, front, own, top, below, out):
    out[...] = front[:, 0]
    for m in range(8):
        t = pos[0, 0, m]

        @pl.when((pos[0, 1, 0] == 0) & (t >= 0))
        def _():
            out[m] += own[t, 0]

        t2 = pos[1, 0, m]

        @pl.when((pos[1, 1, 0] == 0) & (t2 == 0))
        def _():
            out[m] += top[0, 0]

        @pl.when((pos[1, 1, 0] == 0) & (t2 > 0))
        def _():
            out[m] += below[t2 - 1]


def split(x):
    high = x.astype(jnp.bfloat16)
    low = (x - high.astype(jnp.float32)).astype(jnp.bfloat16)
    return high, low


def schur_kernel(
    pos, place, front, own, top, below, row_tiles, high, low, column_part, inverse, diagonal, out,
    panel, right,
):
    step = pl.program_id(0)
    row = place[0]
    column = place[1]
    for k in range(PANELS):
        for m in range(WIDTH):
            panel[k * TILE : (k + 1) * TILE, m * TILE : (m + 1) * TILE] = row_tiles[k, m]
    for at, end in CUTS:
        right[at:end, :] = mul_nn(inverse[at:end, :end], panel[:end, :])
    right_high, right_low = split(right[...])
    update = mul_nn(
        jnp.concatenate([low[...], high[...], high[...]], axis=1),
        jnp.concatenate([right_high, right_low, right_high], axis=0),
        None,
    )
    for l in range(8):
        for m in range(WIDTH):
            out[l, m] = front[l, m] - update[
                l * TILE : (l + 1) * TILE, m * TILE : (m + 1) * TILE
            ]
    for m in range(WIDTH):
        u = pos[0, 1, step * WIDTH + m]
        u2 = pos[1, 1, step * WIDTH + m]
        for l in range(8):
            t = pos[0, 0, l]
            t2 = pos[1, 0, l]

            @pl.when((t >= 0) & (u >= 0))
            def _():
                out[l, m] += own[t, u]

            @pl.when((t2 == 0) & (u2 >= 0))
            def _():
                out[l, m] += top[0, u2]

            @pl.when((t2 > 0) & (u2 >= 0))
            def _():
                out[l, m] += below[t2 - 1, u2]

    @pl.when((step == 0) & (column < PANELS))
    def _():
        for l in range(1, 8):
            out[l, 0] = column_part[l]

        @pl.when((row > column) | (row >= PANELS))
        def _():
            out[0, 0] = column_part[0]

        @pl.when(row == column)
        def _():
            out[0, 0] = diagonal[jnp.minimum(row, PANELS - 1)]

    pivot = jnp.minimum(row, PANELS - 1)
    for m in range(WIDTH):
        first = (step == 0) if m == 0 else False
        skip = jnp.logical_and(first, row >= column)

        @pl.when((row < PANELS) & jnp.logical_not(skip))
        def _():
            here = pl.ds(pl.multiple_of(pivot * TILE, TILE), TILE)
            out[0, m] = right[here, m * TILE : (m + 1) * TILE]


def whole(*shape):
    return pl.BlockSpec(shape, lambda *_: (0,) * len(shape))


def f32(*shape):
    return jax.ShapeDtypeStruct(shape, jnp.float32)


def places(lists, position, count):
    value = jnp.arange(count, dtype=jnp.int32) * 8 + position
    there = jnp.any(lists[:, None, :] == value[None, :, None], axis=2)
    same = (lists % 8 == position)[:, None, :]
    before = jnp.sum((lists[:, None, :] < value[None, :, None]) & same, axis=2, dtype=jnp.int32)
    return jnp.where(there, before, -1)


def sources(column):
    return [(column - slot) % PANELS for slot in range(SLOTS)]


def per_device(front, child_update, child_tiles):
    row_at = lax.axis_index("row")
    col_at = lax.axis_index("col")
    group_at = lax.axis_index("grp")
    local = front[0, 0, :, 0]
    own = child_update[0, 0, 0, :, 0]
    given = child_update[0, 1, 0, :, 0]
    both = ("row", "col")
    limit = pltpu.CompilerParams(vmem_limit_bytes=56 * 1024 * 1024)

    siblings = [(g, g ^ 1) for g in range(4)]
    top = lax.ppermute(given[:1], "grp", siblings)

    lists = jnp.stack([child_tiles[group_at, 0], child_tiles[jnp.bitwise_xor(group_at, 1), 1]])
    pos = jnp.stack([places(lists, row_at, 8), places(lists, col_at, 8)], axis=1)
    place = jnp.stack([row_at, col_at]).astype(jnp.int32)

    tile = pl.pallas_call(
        tile_kernel,
        grid=(1,),
        out_shape=f32(TILE, TILE),
        in_specs=[pl.BlockSpec(memory_space=SMEM)] + [whole(1, 1, TILE, TILE)] * 3,
        out_specs=whole(TILE, TILE),
        name="tile",
    )(pos, local, own, top)
    given, tile = lax.optimization_barrier((given, tile))
    left = lax.ppermute(given[1:, 0], "grp", siblings)
    below = lax.ppermute(given[1:], "grp", siblings)
    row_panel = pl.pallas_call(
        row_kernel,
        grid=(1,),
        out_shape=f32(8, TILE, TILE),
        in_specs=[
            pl.BlockSpec(memory_space=SMEM),
            whole(1, 8, TILE, TILE),
            whole(1, 5, TILE, TILE),
            whole(1, 5, TILE, TILE),
        ],
        out_specs=whole(8, TILE, TILE),
        name="row_panel",
    )(pos, local, own, top)

    found = [tile]
    for away in range(1, 8):
        step = [
            (z * 8 + c, (z + away) % 8 * 8 + c) for c in range(PANELS) for z in sources(c)
        ]
        found.append(lax.ppermute(tile, both, step))
    col_panel = pl.pallas_call(
        col_kernel,
        grid=(1,),
        out_shape=f32(8, TILE, TILE),
        in_specs=[
            pl.BlockSpec(memory_space=SMEM),
            whole(8, 1, TILE, TILE),
            whole(5, 1, TILE, TILE),
            whole(1, 1, TILE, TILE),
            whole(4, TILE, TILE),
        ],
        out_specs=whole(8, TILE, TILE),
        name="col_panel",
    )(pos, local, own, top, left)
    row_panel, col_panel, *found = lax.optimization_barrier((row_panel, col_panel, *found))
    row_tiles = lax.all_gather(row_panel, "row")
    picked = pl.pallas_call(
        pick_kernel,
        out_shape=f32(SLOTS, TILE, TILE),
        in_specs=[pl.BlockSpec(memory_space=SMEM)] + [pl.BlockSpec(memory_space=VMEM)] * 8,
        out_specs=pl.BlockSpec(memory_space=VMEM),
        name="pick",
    )(place, *found)
    across = [(c, c ^ 1) for c in range(8)]
    moved = [
        lax.ppermute(col_panel, "col", [(c, (c + away) % 8) for c in range(PANELS)])
        for away in (2, 4, 6)
    ]
    mine = [picked]
    for away in (2, 4, 6):
        mine.append(
            lax.ppermute(picked, "col", [(c, (c + away) % 8) for c in range(PANELS)])
        )
    mine = jnp.stack(mine)
    other = lax.ppermute(mine, "col", across)
    head_inverse, head_diagonal, rest = pl.pallas_call(
        head_kernel,
        out_shape=[
            f32(HEAD * TILE, LEAD), f32(HEAD, TILE, TILE), f32((PANELS - HEAD) * TILE, LEAD)
        ],
        in_specs=[pl.BlockSpec(memory_space=SMEM)] + [pl.BlockSpec(memory_space=VMEM)] * 2,
        out_specs=[pl.BlockSpec(memory_space=VMEM)] * 3,
        scratch_shapes=[pltpu.VMEM((LEAD, 2 * LEAD), jnp.float32)],
        compiler_params=limit,
        cost_estimate=pl.CostEstimate(
            flops=18_000_000_000, bytes_accessed=6_000_000, transcendentals=0
        ),
        name="head",
    )(place, mine, other)

    *moved, below, head_inverse = lax.optimization_barrier((*moved, below, head_inverse))
    col_mine = [col_panel, *moved]
    col_other = [lax.ppermute(part, "col", across) for part in col_mine]
    inverse, diagonal, high, low, column_part = pl.pallas_call(
        tail_kernel,
        out_shape=[
            f32(LEAD, LEAD),
            f32(PANELS, TILE, TILE),
            jax.ShapeDtypeStruct((8 * TILE, LEAD), jnp.bfloat16),
            jax.ShapeDtypeStruct((8 * TILE, LEAD), jnp.bfloat16),
            f32(8, TILE, TILE),
        ],
        in_specs=[pl.BlockSpec(memory_space=SMEM)] + [pl.BlockSpec(memory_space=VMEM)] * 11,
        out_specs=[pl.BlockSpec(memory_space=VMEM)] * 5,
        scratch_shapes=[
            pltpu.VMEM((LEAD, 2 * LEAD), jnp.float32),
            pltpu.VMEM((8 * TILE, LEAD), jnp.float32),
            pltpu.VMEM((8 * TILE, LEAD), jnp.float32),
        ],
        compiler_params=limit,
        cost_estimate=pl.CostEstimate(
            flops=15_000_000_000, bytes_accessed=6_000_000, transcendentals=0
        ),
        name="tail",
    )(place, rest, head_inverse, head_diagonal, *col_mine, *col_other)

    result = pl.pallas_call(
        schur_kernel,
        grid=(8 // WIDTH,),
        out_shape=f32(8, 8, TILE, TILE),
        in_specs=[
            pl.BlockSpec(memory_space=SMEM),
            pl.BlockSpec(memory_space=SMEM),
            pl.BlockSpec((8, WIDTH, TILE, TILE), lambda i: (0, i, 0, 0)),
            whole(5, 5, TILE, TILE),
            whole(1, 5, TILE, TILE),
            whole(4, 5, TILE, TILE),
            pl.BlockSpec((PANELS, WIDTH, TILE, TILE), lambda i: (0, i, 0, 0)),
            whole(8 * TILE, LEAD),
            whole(8 * TILE, LEAD),
            whole(8, TILE, TILE),
            whole(LEAD, LEAD),
            whole(PANELS, TILE, TILE),
        ],
        out_specs=pl.BlockSpec((8, WIDTH, TILE, TILE), lambda i: (0, i, 0, 0)),
        scratch_shapes=[
            pltpu.VMEM((LEAD, WIDTH * TILE), jnp.float32),
            pltpu.VMEM((LEAD, WIDTH * TILE), jnp.float32),
        ],
        compiler_params=limit,
        name="schur",
    )(
        pos, place, local, own, top, below, row_tiles, high, low, column_part, inverse, diagonal
    )
    return result[None, None, :, None]


def solution(mesh):
    in_specs = (
        P("grp", "row", None, "col", None, None, None),
        P("grp", None, "row", None, "col", None, None, None),
        P(),
    )
    out_specs = P("grp", "row", None, "col", None, None, None)
    return jax.shard_map(
        per_device, mesh=mesh, in_specs=in_specs, out_specs=out_specs, check_vma=False
    )
```

```python
import functools

import jax
import jax.numpy as jnp
from jax import lax
from jax.experimental import pallas as pl
from jax.experimental.pallas import tpu as pltpu
from jax.sharding import PartitionSpec as P

PANELS = 5
TILE = 128
LEAD = PANELS * TILE
BLOCK = 32
SUB = 16
SLOTS = 3
HEAD = 3
LAST = HEAD + 1
WIDTH = 2
CUTS = ((0, 256), (256, 512), (512, 640))
HIGHEST = lax.Precision.HIGHEST
VMEM = pltpu.VMEM
SMEM = pltpu.SMEM


def mul_nn(a, b, precision=HIGHEST):
    return lax.dot_general(
        a, b, (((1,), (0,)), ((), ())), precision=precision, preferred_element_type=jnp.float32
    )


def mul_tn(a, b, precision=HIGHEST):
    return lax.dot_general(
        a, b, (((0,), (0,)), ((), ())), precision=precision, preferred_element_type=jnp.float32
    )


def mul_nt(a, b, precision=HIGHEST):
    return lax.dot_general(
        a, b, (((1,), (1,)), ((), ())), precision=precision, preferred_element_type=jnp.float32
    )


def over_rows(x, at):
    return jnp.broadcast_to(x[at : at + 1, :], (8, TILE))


def eliminate(v, w, base):
    parts = BLOCK // 8
    sub = lax.broadcasted_iota(jnp.int32, (8, TILE), 0)
    scale = [jnp.zeros((8, TILE), jnp.float32) for _ in range(parts)]
    cols = {}
    for j in range(BLOCK):
        top, at = divmod(j, 8)
        group = range(j + 1, (j // SUB + 1) * SUB)
        if j % SUB == 0:
            cols = {
                k: [
                    jnp.broadcast_to(v[h][:, base + k : base + k + 1], (8, TILE))
                    if h >= top
                    else None
                    for h in range(parts)
                ]
                for k in range(j, j + SUB)
            }
        root = lax.rsqrt(over_rows(cols[j][top], at))
        inverse = root * root
        scale[top] = jnp.where(sub == at, root, scale[top])
        v_row = over_rows(v[top], at)
        w_row = over_rows(w[top], at)
        c_row = {k: over_rows(cols[k][top], at) for k in group}
        for h in range(top, parts):
            if h == top and at == 7:
                continue
            factor = cols[j][h] * inverse
            if h == top:
                factor = jnp.where(sub > at, factor, 0.0)
            for k in group:
                cols[k][h] = cols[k][h] - factor * c_row[k]
            v[h] = v[h] - factor * v_row
            w[h] = w[h] - factor * w_row
    upper = jnp.concatenate([x * s for x, s in zip(v, scale)], axis=0)
    lower_inverse = jnp.concatenate([x * s for x, s in zip(w, scale)], axis=0)
    return upper, lower_inverse


def factor_tile(pivot, beside=()):
    beside = list(beside)
    row = lax.broadcasted_iota(jnp.int32, (TILE, TILE), 0)
    col = lax.broadcasted_iota(jnp.int32, (TILE, TILE), 1)
    rest = jnp.concatenate([pivot, (row == col).astype(jnp.float32)], axis=1)
    uppers, inverses = [], []
    blocks = TILE // BLOCK
    share = -(-len(beside) // blocks)
    for base in range(0, TILE, BLOCK):
        for _ in range(min(share, len(beside))):
            beside.pop(0)()
        v = [rest[at : at + 8, :TILE] for at in range(0, BLOCK, 8)]
        w = [rest[at : at + 8, TILE:] for at in range(0, BLOCK, 8)]
        upper, inverse = eliminate(v, w, base)
        uppers.append(upper)
        inverses.append(inverse)
        if base + BLOCK < TILE:
            update = mul_tn(upper, jnp.concatenate([upper, inverse], axis=1))
            rest = rest[BLOCK:] - update[base + BLOCK :]
    upper = jnp.where(row <= col, jnp.concatenate(uppers, axis=0), 0.0)
    inverse = jnp.where(row >= col, jnp.concatenate(inverses, axis=0), 0.0)
    return upper, inverse


def span(at):
    return slice(at * TILE, (at + 1) * TILE)


def advance(work, diagonal, k, beside=(), first=0):
    upper, inverse = factor_tile(work[span(k), span(k)], beside)
    diagonal[k - first] = upper.T
    work[span(k), span(PANELS + k)] = inverse
    at = min(k + 1, PANELS) * TILE
    wide = slice(at, at + (PANELS - 1) * TILE)
    work[span(k), wide] = mul_nn(inverse, work[span(k), wide])
    for i in range(k + 1, PANELS):
        old = slice(i * TILE, LEAD + k * TILE)
        both = mul_tn(work[span(k), span(i)], work[span(k), i * TILE : LEAD + (k + 1) * TILE])
        width = LEAD + k * TILE - i * TILE
        work[span(i), old] = work[span(i), old] - both[:, :width]
        work[span(i), span(PANELS + k)] = -both[:, width:]


def keep_inverse(work, inverse_ref, k):
    done = (k + 1) * TILE
    inverse_ref[span(k), :done] = work[span(k), LEAD : LEAD + done]
    if done < LEAD:
        inverse_ref[span(k), done:] = jnp.zeros((TILE, LEAD - done), jnp.float32)


def head_kernel(place, mine, other, inverse_ref, diagonal_ref, rest_ref, work):
    half = place[1] % 2
    chip = place[1] // 2

    def stored(column, slot):
        away = lax.rem(chip + 4 - column // 2, 4)
        here = mine[away, slot]
        there = other[away, slot]
        return jnp.where(half == column % 2, here, there)

    for k in range(PANELS):
        for i in range(k, PANELS):
            apart = i - k
            if apart < SLOTS:
                tile = stored(i, apart)
            else:
                tile = stored(k, PANELS - apart).T
            work[span(k), span(i)] = tile
    for k in range(HEAD):
        advance(work, diagonal_ref, k)
        keep_inverse(work, inverse_ref, k)
    rest_ref[...] = work[HEAD * TILE :, HEAD * TILE : LEAD + HEAD * TILE]


def middle_kernel(rest, inverse_ref, diagonal_ref, rest_ref, work):
    work[HEAD * TILE :, HEAD * TILE : LEAD + HEAD * TILE] = rest[...]
    advance(work, diagonal_ref, HEAD, first=HEAD)
    inverse_ref[:, : LAST * TILE] = work[span(HEAD), LEAD : LEAD + LAST * TILE]
    inverse_ref[:, LAST * TILE :] = jnp.zeros((TILE, TILE), jnp.float32)
    rest_ref[...] = work[LAST * TILE :, LAST * TILE : LEAD + LAST * TILE]


def tail_kernel(
    place, rest, head_inverse, head_diagonal, middle_inverse, middle_diagonal,
    m0, m1, m2, m3, o0, o1, o2, o3,
    inverse_ref, diagonal_ref, high, low, own_column, work, panel, full,
):
    column = place[1]
    half = column % 2
    chip = column // 2
    for k in range(PANELS):
        away = lax.rem(chip + 4 - k // 2, 4)
        for at, (mine, other) in enumerate(((m0, o0), (m1, o1), (m2, o2), (m3, o3))):

            @pl.when((away == at) & (half == k % 2))
            def _():
                panel[:, k * TILE : (k + 1) * TILE] = mine[...].reshape(8 * TILE, TILE)

            @pl.when((away == at) & (half != k % 2))
            def _():
                panel[:, k * TILE : (k + 1) * TILE] = other[...].reshape(8 * TILE, TILE)

    work[LAST * TILE :, LAST * TILE : LEAD + LAST * TILE] = rest[...]
    inverse_ref[: HEAD * TILE] = head_inverse[...]
    inverse_ref[HEAD * TILE : LAST * TILE] = middle_inverse[...]
    diagonal_ref[:HEAD] = head_diagonal[...]
    diagonal_ref[HEAD] = middle_diagonal[0]

    def product(rows, at, end):
        part = mul_nt(panel[rows, :end], inverse_ref[at:end, :end])
        high[rows, at:end], low[rows, at:end] = split(part)
        full[rows, at:end] = part

    quarters = [slice(at, at + 2 * TILE) for at in range(0, 8 * TILE, 2 * TILE)]
    beside = [
        functools.partial(product, rows, start, stop)
        for start, stop in CUTS[:-1]
        for rows in quarters
    ]
    advance(work, diagonal_ref, LAST, beside)
    keep_inverse(work, inverse_ref, LAST)
    product(slice(0, 8 * TILE), *CUTS[-1])
    wanted = jnp.minimum(column, PANELS - 1)
    for k in range(PANELS):

        @pl.when(wanted == k)
        def _():
            own_column[...] = full[:, k * TILE : (k + 1) * TILE].reshape(8, TILE, TILE)


def pick_kernel(place, *refs):
    *found, out = refs
    for slot in range(SLOTS):
        wanted = lax.rem(place[1] + 2 * PANELS - slot, PANELS)
        away = lax.rem(place[0] + 8 - wanted, 8)
        for at, ref in enumerate(found):

            @pl.when(away == at)
            def _():
                out[slot] = ref[...]


def tile_kernel(pos, front, own, given, out):
    out[...] = front[0, 0]
    for s, child in ((0, own), (1, given)):

        @pl.when((pos[s, 0, 0] == 0) & (pos[s, 1, 0] == 0))
        def _():
            out[...] += child[0, 0]


def row_kernel(pos, front, own, given, out):
    out[...] = front[0]
    for s, child in ((0, own), (1, given)):
        for m in range(8):
            u = pos[s, 1, m]

            @pl.when((pos[s, 0, 0] == 0) & (u >= 0))
            def _():
                out[m] += child[0, u]


def col_kernel(pos, front, own, top, below, out):
    out[...] = front[:, 0]
    for m in range(8):
        t = pos[0, 0, m]

        @pl.when((pos[0, 1, 0] == 0) & (t >= 0))
        def _():
            out[m] += own[t, 0]

        t2 = pos[1, 0, m]

        @pl.when((pos[1, 1, 0] == 0) & (t2 == 0))
        def _():
            out[m] += top[0, 0]

        @pl.when((pos[1, 1, 0] == 0) & (t2 > 0))
        def _():
            out[m] += below[t2 - 1]


def split(x):
    high = x.astype(jnp.bfloat16)
    low = (x - high.astype(jnp.float32)).astype(jnp.bfloat16)
    return high, low


def schur_kernel(
    pos, place, front, own, top, below, row_tiles, high, low, column_part, inverse, diagonal, out,
    panel, right,
):
    step = pl.program_id(0)
    row = place[0]
    column = place[1]
    for k in range(PANELS):
        for m in range(WIDTH):
            panel[k * TILE : (k + 1) * TILE, m * TILE : (m + 1) * TILE] = row_tiles[k, m]
    for at, end in CUTS:
        right[at:end, :] = mul_nn(inverse[at:end, :end], panel[:end, :])
    right_high, right_low = split(right[...])
    update = mul_nn(
        jnp.concatenate([low[...], high[...], high[...]], axis=1),
        jnp.concatenate([right_high, right_low, right_high], axis=0),
        None,
    )
    for l in range(8):
        for m in range(WIDTH):
            out[l, m] = front[l, m] - update[
                l * TILE : (l + 1) * TILE, m * TILE : (m + 1) * TILE
            ]
    for m in range(WIDTH):
        u = pos[0, 1, step * WIDTH + m]
        u2 = pos[1, 1, step * WIDTH + m]
        for l in range(8):
            t = pos[0, 0, l]
            t2 = pos[1, 0, l]

            @pl.when((t >= 0) & (u >= 0))
            def _():
                out[l, m] += own[t, u]

            @pl.when((t2 == 0) & (u2 >= 0))
            def _():
                out[l, m] += top[0, u2]

            @pl.when((t2 > 0) & (u2 >= 0))
            def _():
                out[l, m] += below[t2 - 1, u2]

    @pl.when((step == 0) & (column < PANELS))
    def _():
        for l in range(1, 8):
            out[l, 0] = column_part[l]

        @pl.when((row > column) | (row >= PANELS))
        def _():
            out[0, 0] = column_part[0]

        @pl.when(row == column)
        def _():
            out[0, 0] = diagonal[jnp.minimum(row, PANELS - 1)]

    pivot = jnp.minimum(row, PANELS - 1)
    for m in range(WIDTH):
        first = (step == 0) if m == 0 else False
        skip = jnp.logical_and(first, row >= column)

        @pl.when((row < PANELS) & jnp.logical_not(skip))
        def _():
            here = pl.ds(pl.multiple_of(pivot * TILE, TILE), TILE)
            out[0, m] = right[here, m * TILE : (m + 1) * TILE]


def whole(*shape):
    return pl.BlockSpec(shape, lambda *_: (0,) * len(shape))


def f32(*shape):
    return jax.ShapeDtypeStruct(shape, jnp.float32)


def places(lists, position, count):
    value = jnp.arange(count, dtype=jnp.int32) * 8 + position
    there = jnp.any(lists[:, None, :] == value[None, :, None], axis=2)
    same = (lists % 8 == position)[:, None, :]
    before = jnp.sum((lists[:, None, :] < value[None, :, None]) & same, axis=2, dtype=jnp.int32)
    return jnp.where(there, before, -1)


def sources(column):
    return [(column - slot) % PANELS for slot in range(SLOTS)]


def per_device(front, child_update, child_tiles):
    row_at = lax.axis_index("row")
    col_at = lax.axis_index("col")
    group_at = lax.axis_index("grp")
    local = front[0, 0, :, 0]
    own = child_update[0, 0, 0, :, 0]
    given = child_update[0, 1, 0, :, 0]
    both = ("row", "col")
    limit = pltpu.CompilerParams(vmem_limit_bytes=36 * 1024 * 1024)
    most = pltpu.CompilerParams(vmem_limit_bytes=50 * 1024 * 1024)

    siblings = [(g, g ^ 1) for g in range(4)]
    top = lax.ppermute(given[:1], "grp", siblings)

    lists = jnp.stack([child_tiles[group_at, 0], child_tiles[jnp.bitwise_xor(group_at, 1), 1]])
    pos = jnp.stack([places(lists, row_at, 8), places(lists, col_at, 8)], axis=1)
    place = jnp.stack([row_at, col_at]).astype(jnp.int32)

    tile = pl.pallas_call(
        tile_kernel,
        grid=(1,),
        out_shape=f32(TILE, TILE),
        in_specs=[pl.BlockSpec(memory_space=SMEM)] + [whole(1, 1, TILE, TILE)] * 3,
        out_specs=whole(TILE, TILE),
        name="tile",
    )(pos, local, own, top)
    given, tile = lax.optimization_barrier((given, tile))
    left = lax.ppermute(given[1:, 0], "grp", siblings)
    below = lax.ppermute(given[1:], "grp", siblings)
    row_panel = pl.pallas_call(
        row_kernel,
        grid=(1,),
        out_shape=f32(8, TILE, TILE),
        in_specs=[
            pl.BlockSpec(memory_space=SMEM),
            whole(1, 8, TILE, TILE),
            whole(1, 5, TILE, TILE),
            whole(1, 5, TILE, TILE),
        ],
        out_specs=whole(8, TILE, TILE),
        name="row_panel",
    )(pos, local, own, top)

    found = [tile]
    for away in range(1, 8):
        step = [
            (z * 8 + c, (z + away) % 8 * 8 + c) for c in range(PANELS) for z in sources(c)
        ]
        found.append(lax.ppermute(tile, both, step))
    row_panel, left, *found = lax.optimization_barrier((row_panel, left, *found))
    row_tiles = lax.all_gather(row_panel, "row")
    picked = pl.pallas_call(
        pick_kernel,
        out_shape=f32(SLOTS, TILE, TILE),
        in_specs=[pl.BlockSpec(memory_space=SMEM)] + [pl.BlockSpec(memory_space=VMEM)] * 8,
        out_specs=pl.BlockSpec(memory_space=VMEM),
        name="pick",
    )(place, *found)
    across = [(c, c ^ 1) for c in range(8)]
    col_panel = pl.pallas_call(
        col_kernel,
        grid=(1,),
        out_shape=f32(8, TILE, TILE),
        in_specs=[
            pl.BlockSpec(memory_space=SMEM),
            whole(8, 1, TILE, TILE),
            whole(5, 1, TILE, TILE),
            whole(1, 1, TILE, TILE),
            whole(4, TILE, TILE),
        ],
        out_specs=whole(8, TILE, TILE),
        name="col_panel",
    )(pos, local, own, top, left)
    mine = [picked]
    for away in (2, 4, 6):
        mine.append(
            lax.ppermute(picked, "col", [(c, (c + away) % 8) for c in range(PANELS)])
        )
    *mine, col_panel = lax.optimization_barrier((*mine, col_panel))
    mine = jnp.stack(mine)
    moved = [
        lax.ppermute(col_panel, "col", [(c, (c + away) % 8) for c in range(PANELS)])
        for away in (2, 4, 6)
    ]
    other = lax.ppermute(mine, "col", across)
    head_inverse, head_diagonal, rest = pl.pallas_call(
        head_kernel,
        out_shape=[
            f32(HEAD * TILE, LEAD), f32(HEAD, TILE, TILE), f32((PANELS - HEAD) * TILE, LEAD)
        ],
        in_specs=[pl.BlockSpec(memory_space=SMEM)] + [pl.BlockSpec(memory_space=VMEM)] * 2,
        out_specs=[pl.BlockSpec(memory_space=VMEM)] * 3,
        scratch_shapes=[pltpu.VMEM((LEAD, 2 * LEAD), jnp.float32)],
        compiler_params=limit,
        cost_estimate=pl.CostEstimate(
            flops=18_000_000_000, bytes_accessed=6_000_000, transcendentals=0
        ),
        name="head",
    )(place, mine, other)

    *moved, rest = lax.optimization_barrier((*moved, rest))
    col_mine = [col_panel, *moved]
    col_other = [lax.ppermute(part, "col", across) for part in col_mine]
    middle_inverse, middle_diagonal, rest = pl.pallas_call(
        middle_kernel,
        out_shape=[f32(TILE, LEAD), f32(1, TILE, TILE), f32(TILE, LEAD)],
        in_specs=[pl.BlockSpec(memory_space=VMEM)],
        out_specs=[pl.BlockSpec(memory_space=VMEM)] * 3,
        scratch_shapes=[pltpu.VMEM((LEAD, 2 * LEAD), jnp.float32)],
        compiler_params=limit,
        cost_estimate=pl.CostEstimate(
            flops=6_000_000_000, bytes_accessed=2_000_000, transcendentals=0
        ),
        name="middle",
    )(rest)
    below, rest = lax.optimization_barrier((below, rest))
    inverse, diagonal, high, low, column_part = pl.pallas_call(
        tail_kernel,
        out_shape=[
            f32(LEAD, LEAD),
            f32(PANELS, TILE, TILE),
            jax.ShapeDtypeStruct((8 * TILE, LEAD), jnp.bfloat16),
            jax.ShapeDtypeStruct((8 * TILE, LEAD), jnp.bfloat16),
            f32(8, TILE, TILE),
        ],
        in_specs=[pl.BlockSpec(memory_space=SMEM)] + [pl.BlockSpec(memory_space=VMEM)] * 13,
        out_specs=[pl.BlockSpec(memory_space=VMEM)] * 5,
        scratch_shapes=[
            pltpu.VMEM((LEAD, 2 * LEAD), jnp.float32),
            pltpu.VMEM((8 * TILE, LEAD), jnp.float32),
            pltpu.VMEM((8 * TILE, LEAD), jnp.float32),
        ],
        compiler_params=limit,
        cost_estimate=pl.CostEstimate(
            flops=9_000_000_000, bytes_accessed=6_000_000, transcendentals=0
        ),
        name="tail",
    )(place, rest, head_inverse, head_diagonal, middle_inverse, middle_diagonal, *col_mine, *col_other)

    result = pl.pallas_call(
        schur_kernel,
        grid=(8 // WIDTH,),
        out_shape=f32(8, 8, TILE, TILE),
        in_specs=[
            pl.BlockSpec(memory_space=SMEM),
            pl.BlockSpec(memory_space=SMEM),
            pl.BlockSpec((8, WIDTH, TILE, TILE), lambda i: (0, i, 0, 0)),
            whole(5, 5, TILE, TILE),
            whole(1, 5, TILE, TILE),
            whole(4, 5, TILE, TILE),
            pl.BlockSpec((PANELS, WIDTH, TILE, TILE), lambda i: (0, i, 0, 0)),
            whole(8 * TILE, LEAD),
            whole(8 * TILE, LEAD),
            whole(8, TILE, TILE),
            whole(LEAD, LEAD),
            whole(PANELS, TILE, TILE),
        ],
        out_specs=pl.BlockSpec((8, WIDTH, TILE, TILE), lambda i: (0, i, 0, 0)),
        scratch_shapes=[
            pltpu.VMEM((LEAD, WIDTH * TILE), jnp.float32),
            pltpu.VMEM((LEAD, WIDTH * TILE), jnp.float32),
        ],
        compiler_params=most,
        name="schur",
    )(
        pos, place, local, own, top, below, row_tiles, high, low, column_part, inverse, diagonal
    )
    return result[None, None, :, None]


def solution(mesh):
    in_specs = (
        P("grp", "row", None, "col", None, None, None),
        P("grp", None, "row", None, "col", None, None, None),
        P(),
    )
    out_specs = P("grp", "row", None, "col", None, None, None)
    return jax.shard_map(
        per_device, mesh=mesh, in_specs=in_specs, out_specs=out_specs, check_vma=False
    )
```

```python
import functools

import jax
import jax.numpy as jnp
from jax import lax
from jax.experimental import pallas as pl
from jax.experimental.pallas import tpu as pltpu
from jax.sharding import PartitionSpec as P

PANELS = 5
TILE = 128
LEAD = PANELS * TILE
BLOCK = 32
SUB = 16
SLOTS = 3
HEAD = 3
LAST = HEAD + 1
WIDTH = 2
CUTS = ((0, 256), (256, 512), (512, 640))
HIGHEST = lax.Precision.HIGHEST
VMEM = pltpu.VMEM
SMEM = pltpu.SMEM


def mul_nn(a, b, precision=HIGHEST):
    return lax.dot_general(
        a, b, (((1,), (0,)), ((), ())), precision=precision, preferred_element_type=jnp.float32
    )


def mul_tn(a, b, precision=HIGHEST):
    return lax.dot_general(
        a, b, (((0,), (0,)), ((), ())), precision=precision, preferred_element_type=jnp.float32
    )


def mul_nt(a, b, precision=HIGHEST):
    return lax.dot_general(
        a, b, (((1,), (1,)), ((), ())), precision=precision, preferred_element_type=jnp.float32
    )


def over_rows(x, at):
    return jnp.broadcast_to(x[at : at + 1, :], (8, TILE))


def eliminate(v, w, base):
    parts = BLOCK // 8
    sub = lax.broadcasted_iota(jnp.int32, (8, TILE), 0)
    scale = [jnp.zeros((8, TILE), jnp.float32) for _ in range(parts)]
    cols = {}
    for j in range(BLOCK):
        top, at = divmod(j, 8)
        group = range(j + 1, (j // SUB + 1) * SUB)
        if j % SUB == 0:
            cols = {
                k: [
                    jnp.broadcast_to(v[h][:, base + k : base + k + 1], (8, TILE))
                    if h >= top
                    else None
                    for h in range(parts)
                ]
                for k in range(j, j + SUB)
            }
        root = lax.rsqrt(over_rows(cols[j][top], at))
        inverse = root * root
        scale[top] = jnp.where(sub == at, root, scale[top])
        v_row = over_rows(v[top], at)
        w_row = over_rows(w[top], at)
        c_row = {k: over_rows(cols[k][top], at) for k in group}
        for h in range(top, parts):
            if h == top and at == 7:
                continue
            factor = cols[j][h] * inverse
            if h == top:
                factor = jnp.where(sub > at, factor, 0.0)
            for k in group:
                cols[k][h] = cols[k][h] - factor * c_row[k]
            v[h] = v[h] - factor * v_row
            w[h] = w[h] - factor * w_row
    upper = jnp.concatenate([x * s for x, s in zip(v, scale)], axis=0)
    lower_inverse = jnp.concatenate([x * s for x, s in zip(w, scale)], axis=0)
    return upper, lower_inverse


def factor_tile(pivot, beside=()):
    beside = list(beside)
    row = lax.broadcasted_iota(jnp.int32, (TILE, TILE), 0)
    col = lax.broadcasted_iota(jnp.int32, (TILE, TILE), 1)
    rest = jnp.concatenate([pivot, (row == col).astype(jnp.float32)], axis=1)
    uppers, inverses = [], []
    blocks = TILE // BLOCK
    share = -(-len(beside) // blocks)
    for base in range(0, TILE, BLOCK):
        for _ in range(min(share, len(beside))):
            beside.pop(0)()
        v = [rest[at : at + 8, :TILE] for at in range(0, BLOCK, 8)]
        w = [rest[at : at + 8, TILE:] for at in range(0, BLOCK, 8)]
        upper, inverse = eliminate(v, w, base)
        uppers.append(upper)
        inverses.append(inverse)
        if base + BLOCK < TILE:
            update = mul_tn(upper, jnp.concatenate([upper, inverse], axis=1))
            rest = rest[BLOCK:] - update[base + BLOCK :]
    upper = jnp.where(row <= col, jnp.concatenate(uppers, axis=0), 0.0)
    inverse = jnp.where(row >= col, jnp.concatenate(inverses, axis=0), 0.0)
    return upper, inverse


def span(at):
    return slice(at * TILE, (at + 1) * TILE)


def advance(work, diagonal, k, beside=(), first=0):
    upper, inverse = factor_tile(work[span(k), span(k)], beside)
    diagonal[k - first] = upper.T
    work[span(k), span(PANELS + k)] = inverse
    at = min(k + 1, PANELS) * TILE
    wide = slice(at, at + (PANELS - 1) * TILE)
    work[span(k), wide] = mul_nn(inverse, work[span(k), wide])
    for i in range(k + 1, PANELS):
        old = slice(i * TILE, LEAD + k * TILE)
        both = mul_tn(work[span(k), span(i)], work[span(k), i * TILE : LEAD + (k + 1) * TILE])
        width = LEAD + k * TILE - i * TILE
        work[span(i), old] = work[span(i), old] - both[:, :width]
        work[span(i), span(PANELS + k)] = -both[:, width:]


def keep_inverse(work, inverse_ref, k):
    done = (k + 1) * TILE
    inverse_ref[span(k), :done] = work[span(k), LEAD : LEAD + done]
    if done < LEAD:
        inverse_ref[span(k), done:] = jnp.zeros((TILE, LEAD - done), jnp.float32)


def head_kernel(place, mine, other, inverse_ref, diagonal_ref, rest_ref, work):
    half = place[1] % 2
    chip = place[1] // 2

    def stored(column, slot):
        away = lax.rem(chip + 4 - column // 2, 4)
        here = mine[away, slot]
        there = other[away, slot]
        return jnp.where(half == column % 2, here, there)

    for k in range(PANELS):
        for i in range(k, PANELS):
            apart = i - k
            if apart < SLOTS:
                tile = stored(i, apart)
            else:
                tile = stored(k, PANELS - apart).T
            work[span(k), span(i)] = tile
    for k in range(HEAD):
        advance(work, diagonal_ref, k)
        keep_inverse(work, inverse_ref, k)
    rest_ref[...] = work[HEAD * TILE :, HEAD * TILE : LEAD + HEAD * TILE]


def middle_kernel(rest, inverse_ref, diagonal_ref, rest_ref, work):
    work[HEAD * TILE :, HEAD * TILE : LEAD + HEAD * TILE] = rest[...]
    advance(work, diagonal_ref, HEAD, first=HEAD)
    inverse_ref[:, : LAST * TILE] = work[span(HEAD), LEAD : LEAD + LAST * TILE]
    inverse_ref[:, LAST * TILE :] = jnp.zeros((TILE, TILE), jnp.float32)
    rest_ref[...] = work[LAST * TILE :, LAST * TILE : LEAD + LAST * TILE]


def tail_kernel(
    place, rest, head_inverse, head_diagonal, middle_inverse, middle_diagonal,
    m0, m1, m2, m3, o0, o1, o2, o3,
    inverse_ref, diagonal_ref, high, low, own_column, work, panel, full,
):
    column = place[1]
    half = column % 2
    chip = column // 2
    for k in range(PANELS):
        away = lax.rem(chip + 4 - k // 2, 4)
        for at, (mine, other) in enumerate(((m0, o0), (m1, o1), (m2, o2), (m3, o3))):

            @pl.when((away == at) & (half == k % 2))
            def _():
                panel[:, k * TILE : (k + 1) * TILE] = mine[...].reshape(8 * TILE, TILE)

            @pl.when((away == at) & (half != k % 2))
            def _():
                panel[:, k * TILE : (k + 1) * TILE] = other[...].reshape(8 * TILE, TILE)

    work[LAST * TILE :, LAST * TILE : LEAD + LAST * TILE] = rest[...]
    inverse_ref[: HEAD * TILE] = head_inverse[...]
    inverse_ref[HEAD * TILE : LAST * TILE] = middle_inverse[...]
    diagonal_ref[:HEAD] = head_diagonal[...]
    diagonal_ref[HEAD] = middle_diagonal[0]

    def product(rows, at, end):
        part = mul_nt(panel[rows, :end], inverse_ref[at:end, :end])
        high[rows, at:end], low[rows, at:end] = split(part)
        full[rows, at:end] = part

    quarters = [slice(at, at + 2 * TILE) for at in range(0, 8 * TILE, 2 * TILE)]
    beside = [
        functools.partial(product, rows, start, stop)
        for start, stop in CUTS[:-1]
        for rows in quarters
    ]
    done = LAST * TILE

    def reduce(rows):
        known = work[span(LAST), LEAD : LEAD + done]
        full[rows, done:] = panel[rows, done:] + mul_nt(panel[rows, :done], known)

    beside += [functools.partial(reduce, rows) for rows in quarters]
    advance(work, diagonal_ref, LAST, beside)
    keep_inverse(work, inverse_ref, LAST)
    part = mul_nt(full[:, done:], inverse_ref[done:, done:])
    high[:, done:], low[:, done:] = split(part)
    full[:, done:] = part
    wanted = jnp.minimum(column, PANELS - 1)
    for k in range(PANELS):

        @pl.when(wanted == k)
        def _():
            own_column[...] = full[:, k * TILE : (k + 1) * TILE].reshape(8, TILE, TILE)


def pick_kernel(place, *refs):
    *found, out = refs
    for slot in range(SLOTS):
        wanted = lax.rem(place[1] + 2 * PANELS - slot, PANELS)
        away = lax.rem(place[0] + 8 - wanted, 8)
        for at, ref in enumerate(found):

            @pl.when(away == at)
            def _():
                out[slot] = ref[...]


def tile_kernel(pos, front, own, given, out):
    out[...] = front[0, 0]
    for s, child in ((0, own), (1, given)):

        @pl.when((pos[s, 0, 0] == 0) & (pos[s, 1, 0] == 0))
        def _():
            out[...] += child[0, 0]


def row_kernel(pos, front, own, given, out):
    out[...] = front[0]
    for s, child in ((0, own), (1, given)):
        for m in range(8):
            u = pos[s, 1, m]

            @pl.when((pos[s, 0, 0] == 0) & (u >= 0))
            def _():
                out[m] += child[0, u]


def col_kernel(pos, front, own, top, below, out):
    out[...] = front[:, 0]
    for m in range(8):
        t = pos[0, 0, m]

        @pl.when((pos[0, 1, 0] == 0) & (t >= 0))
        def _():
            out[m] += own[t, 0]

        t2 = pos[1, 0, m]

        @pl.when((pos[1, 1, 0] == 0) & (t2 == 0))
        def _():
            out[m] += top[0, 0]

        @pl.when((pos[1, 1, 0] == 0) & (t2 > 0))
        def _():
            out[m] += below[t2 - 1]


def split(x):
    high = x.astype(jnp.bfloat16)
    low = (x - high.astype(jnp.float32)).astype(jnp.bfloat16)
    return high, low


def schur_kernel(
    pos, place, front, own, top, below, row_tiles, high, low, column_part, inverse, diagonal, out,
    panel, right,
):
    step = pl.program_id(0)
    row = place[0]
    column = place[1]
    for k in range(PANELS):
        for m in range(WIDTH):
            panel[k * TILE : (k + 1) * TILE, m * TILE : (m + 1) * TILE] = row_tiles[k, m]
    for at, end in CUTS:
        right[at:end, :] = mul_nn(inverse[at:end, :end], panel[:end, :])
    right_high, right_low = split(right[...])
    update = mul_nn(
        jnp.concatenate([low[...], high[...], high[...]], axis=1),
        jnp.concatenate([right_high, right_low, right_high], axis=0),
        None,
    )
    for l in range(8):
        for m in range(WIDTH):
            out[l, m] = front[l, m] - update[
                l * TILE : (l + 1) * TILE, m * TILE : (m + 1) * TILE
            ]
    for m in range(WIDTH):
        u = pos[0, 1, step * WIDTH + m]
        u2 = pos[1, 1, step * WIDTH + m]
        for l in range(8):
            t = pos[0, 0, l]
            t2 = pos[1, 0, l]

            @pl.when((t >= 0) & (u >= 0))
            def _():
                out[l, m] += own[t, u]

            @pl.when((t2 == 0) & (u2 >= 0))
            def _():
                out[l, m] += top[0, u2]

            @pl.when((t2 > 0) & (u2 >= 0))
            def _():
                out[l, m] += below[t2 - 1, u2]

    @pl.when((step == 0) & (column < PANELS))
    def _():
        for l in range(1, 8):
            out[l, 0] = column_part[l]

        @pl.when((row > column) | (row >= PANELS))
        def _():
            out[0, 0] = column_part[0]

        @pl.when(row == column)
        def _():
            out[0, 0] = diagonal[jnp.minimum(row, PANELS - 1)]

    pivot = jnp.minimum(row, PANELS - 1)
    for m in range(WIDTH):
        first = (step == 0) if m == 0 else False
        skip = jnp.logical_and(first, row >= column)

        @pl.when((row < PANELS) & jnp.logical_not(skip))
        def _():
            here = pl.ds(pl.multiple_of(pivot * TILE, TILE), TILE)
            out[0, m] = right[here, m * TILE : (m + 1) * TILE]


def whole(*shape):
    return pl.BlockSpec(shape, lambda *_: (0,) * len(shape))


def f32(*shape):
    return jax.ShapeDtypeStruct(shape, jnp.float32)


def places(lists, position, count):
    value = jnp.arange(count, dtype=jnp.int32) * 8 + position
    there = jnp.any(lists[:, None, :] == value[None, :, None], axis=2)
    same = (lists % 8 == position)[:, None, :]
    before = jnp.sum((lists[:, None, :] < value[None, :, None]) & same, axis=2, dtype=jnp.int32)
    return jnp.where(there, before, -1)


def sources(column):
    return [(column - slot) % PANELS for slot in range(SLOTS)]


def per_device(front, child_update, child_tiles):
    row_at = lax.axis_index("row")
    col_at = lax.axis_index("col")
    group_at = lax.axis_index("grp")
    local = front[0, 0, :, 0]
    own = child_update[0, 0, 0, :, 0]
    given = child_update[0, 1, 0, :, 0]
    both = ("row", "col")
    limit = pltpu.CompilerParams(vmem_limit_bytes=36 * 1024 * 1024)
    most = pltpu.CompilerParams(vmem_limit_bytes=50 * 1024 * 1024)

    siblings = [(g, g ^ 1) for g in range(4)]
    top = lax.ppermute(given[:1], "grp", siblings)

    lists = jnp.stack([child_tiles[group_at, 0], child_tiles[jnp.bitwise_xor(group_at, 1), 1]])
    pos = jnp.stack([places(lists, row_at, 8), places(lists, col_at, 8)], axis=1)
    place = jnp.stack([row_at, col_at]).astype(jnp.int32)

    tile = pl.pallas_call(
        tile_kernel,
        grid=(1,),
        out_shape=f32(TILE, TILE),
        in_specs=[pl.BlockSpec(memory_space=SMEM)] + [whole(1, 1, TILE, TILE)] * 3,
        out_specs=whole(TILE, TILE),
        name="tile",
    )(pos, local, own, top)
    given, tile = lax.optimization_barrier((given, tile))
    left = lax.ppermute(given[1:, 0], "grp", siblings)
    below = lax.ppermute(given[1:], "grp", siblings)
    row_panel = pl.pallas_call(
        row_kernel,
        grid=(1,),
        out_shape=f32(8, TILE, TILE),
        in_specs=[
            pl.BlockSpec(memory_space=SMEM),
            whole(1, 8, TILE, TILE),
            whole(1, 5, TILE, TILE),
            whole(1, 5, TILE, TILE),
        ],
        out_specs=whole(8, TILE, TILE),
        name="row_panel",
    )(pos, local, own, top)

    found = [tile]
    for away in range(1, 8):
        step = [
            (z * 8 + c, (z + away) % 8 * 8 + c) for c in range(PANELS) for z in sources(c)
        ]
        found.append(lax.ppermute(tile, both, step))
    row_panel, left, *found = lax.optimization_barrier((row_panel, left, *found))
    row_tiles = lax.all_gather(row_panel, "row")
    picked = pl.pallas_call(
        pick_kernel,
        out_shape=f32(SLOTS, TILE, TILE),
        in_specs=[pl.BlockSpec(memory_space=SMEM)] + [pl.BlockSpec(memory_space=VMEM)] * 8,
        out_specs=pl.BlockSpec(memory_space=VMEM),
        name="pick",
    )(place, *found)
    across = [(c, c ^ 1) for c in range(8)]
    col_panel = pl.pallas_call(
        col_kernel,
        grid=(1,),
        out_shape=f32(8, TILE, TILE),
        in_specs=[
            pl.BlockSpec(memory_space=SMEM),
            whole(8, 1, TILE, TILE),
            whole(5, 1, TILE, TILE),
            whole(1, 1, TILE, TILE),
            whole(4, TILE, TILE),
        ],
        out_specs=whole(8, TILE, TILE),
        name="col_panel",
    )(pos, local, own, top, left)
    mine = [picked]
    for away in (2, 4, 6):
        mine.append(
            lax.ppermute(picked, "col", [(c, (c + away) % 8) for c in range(PANELS)])
        )
    *mine, col_panel = lax.optimization_barrier((*mine, col_panel))
    mine = jnp.stack(mine)
    moved = [
        lax.ppermute(col_panel, "col", [(c, (c + away) % 8) for c in range(PANELS)])
        for away in (2, 4, 6)
    ]
    other = lax.ppermute(mine, "col", across)
    head_inverse, head_diagonal, rest = pl.pallas_call(
        head_kernel,
        out_shape=[
            f32(HEAD * TILE, LEAD), f32(HEAD, TILE, TILE), f32((PANELS - HEAD) * TILE, LEAD)
        ],
        in_specs=[pl.BlockSpec(memory_space=SMEM)] + [pl.BlockSpec(memory_space=VMEM)] * 2,
        out_specs=[pl.BlockSpec(memory_space=VMEM)] * 3,
        scratch_shapes=[pltpu.VMEM((LEAD, 2 * LEAD), jnp.float32)],
        compiler_params=limit,
        cost_estimate=pl.CostEstimate(
            flops=18_000_000_000, bytes_accessed=6_000_000, transcendentals=0
        ),
        name="head",
    )(place, mine, other)

    *moved, rest = lax.optimization_barrier((*moved, rest))
    col_mine = [col_panel, *moved]
    col_other = [lax.ppermute(part, "col", across) for part in col_mine]
    middle_inverse, middle_diagonal, rest = pl.pallas_call(
        middle_kernel,
        out_shape=[f32(TILE, LEAD), f32(1, TILE, TILE), f32(TILE, LEAD)],
        in_specs=[pl.BlockSpec(memory_space=VMEM)],
        out_specs=[pl.BlockSpec(memory_space=VMEM)] * 3,
        scratch_shapes=[pltpu.VMEM((LEAD, 2 * LEAD), jnp.float32)],
        compiler_params=limit,
        cost_estimate=pl.CostEstimate(
            flops=6_000_000_000, bytes_accessed=2_000_000, transcendentals=0
        ),
        name="middle",
    )(rest)
    below, rest = lax.optimization_barrier((below, rest))
    inverse, diagonal, high, low, column_part = pl.pallas_call(
        tail_kernel,
        out_shape=[
            f32(LEAD, LEAD),
            f32(PANELS, TILE, TILE),
            jax.ShapeDtypeStruct((8 * TILE, LEAD), jnp.bfloat16),
            jax.ShapeDtypeStruct((8 * TILE, LEAD), jnp.bfloat16),
            f32(8, TILE, TILE),
        ],
        in_specs=[pl.BlockSpec(memory_space=SMEM)] + [pl.BlockSpec(memory_space=VMEM)] * 13,
        out_specs=[pl.BlockSpec(memory_space=VMEM)] * 5,
        scratch_shapes=[
            pltpu.VMEM((LEAD, 2 * LEAD), jnp.float32),
            pltpu.VMEM((8 * TILE, LEAD), jnp.float32),
            pltpu.VMEM((8 * TILE, LEAD), jnp.float32),
        ],
        compiler_params=limit,
        cost_estimate=pl.CostEstimate(
            flops=9_000_000_000, bytes_accessed=6_000_000, transcendentals=0
        ),
        name="tail",
    )(place, rest, head_inverse, head_diagonal, middle_inverse, middle_diagonal, *col_mine, *col_other)

    result = pl.pallas_call(
        schur_kernel,
        grid=(8 // WIDTH,),
        out_shape=f32(8, 8, TILE, TILE),
        in_specs=[
            pl.BlockSpec(memory_space=SMEM),
            pl.BlockSpec(memory_space=SMEM),
            pl.BlockSpec((8, WIDTH, TILE, TILE), lambda i: (0, i, 0, 0)),
            whole(5, 5, TILE, TILE),
            whole(1, 5, TILE, TILE),
            whole(4, 5, TILE, TILE),
            pl.BlockSpec((PANELS, WIDTH, TILE, TILE), lambda i: (0, i, 0, 0)),
            whole(8 * TILE, LEAD),
            whole(8 * TILE, LEAD),
            whole(8, TILE, TILE),
            whole(LEAD, LEAD),
            whole(PANELS, TILE, TILE),
        ],
        out_specs=pl.BlockSpec((8, WIDTH, TILE, TILE), lambda i: (0, i, 0, 0)),
        scratch_shapes=[
            pltpu.VMEM((LEAD, WIDTH * TILE), jnp.float32),
            pltpu.VMEM((LEAD, WIDTH * TILE), jnp.float32),
        ],
        compiler_params=most,
        name="schur",
    )(
        pos, place, local, own, top, below, row_tiles, high, low, column_part, inverse, diagonal
    )
    return result[None, None, :, None]


def solution(mesh):
    in_specs = (
        P("grp", "row", None, "col", None, None, None),
        P("grp", None, "row", None, "col", None, None, None),
        P(),
    )
    out_specs = P("grp", "row", None, "col", None, None, None)
    return jax.shard_map(
        per_device, mesh=mesh, in_specs=in_specs, out_specs=out_specs, check_vma=False
    )
```
